32 devices in a mesh: slides: 2 (over x), seq: 16 (over z, y, core).
Axes of the slice: x: 2, y: 2, z: 4, core: 2. Of those that a mesh axis runs over, the one named last changes fastest.
Arguments:
- tiles: bfloat16 [16384, 768], P(('slides', 'seq')), parts along dimension 0, may hold values from -6 to 6
- tile_count: int32 [2], P('slides'), parts along dimension 0, may hold values from 4096 to 8192
- conv_weight: float32 [25, 768], replicated, may hold values from -3 to 3
- conv_bias: float32 [768], replicated, may hold values from -3 to 3
- ln_gain: float32 [768], replicated, may hold values from 0.1 to 1.9
- w_qkv: bfloat16 [768, 2304], replicated, may hold values from -5 to 5
- w_out: bfloat16 [768, 768], replicated, may hold values from -0.21875 to 0.21875
Outputs:
- attended: bfloat16 [16384, 768], P(('slides', 'seq')), parts along dimension 0
- encoded: bfloat16 [16384, 768], P(('slides', 'seq')), parts along dimension 0
The draws below stay inside these ranges and needn't reach their ends.
There are 2 independent parts, one for each index of `slides`. The reference program is written for one: setup_inputs(seed, part) draws one part's arguments, and reference() takes and returns one part's arrays. A program takes and returns all parts, laid end to end along the dimension named above; an argument that names none is the same for every part. Nothing has to cross between parts.
All inputs are finite; a program needn't handle non-finite values.
Results may differ from the reference program's by a relative error of at most 0.0051.
Values may be sent and summed in bfloat16 or wider, within the bound.
A program may use at most 128 MiB of HBM per device.

```python
import jax
import jax.numpy as jnp
from jax import lax

D = 768
ATTENTION_HEADS = 16
HD = 48
TOK_DEV = 512
GW = 128
MID_RATE = 8
FAR_RATE = 16
TOKENS = 8192


def draw_w_qkv(key, part):
    first_key = jax.random.fold_in(key, 0)
    base = jax.random.truncated_normal(first_key, -4.0, 4.0, (D, 3 * D), jnp.float32) * D ** (-0.5)
    return base.astype(jnp.bfloat16)


def block_scale(rng, shape, shards, smallest, high):
    def one(axis_at, blocks):
        steps = jax.random.uniform(jax.random.fold_in(jax.random.fold_in(rng, 6), axis_at), (blocks,), jnp.float32, smallest / len(shards), high / len(shards))
        return jnp.repeat(jnp.exp(steps), shape[axis_at] // blocks).reshape((-1,) + (1,) * (len(shape) - axis_at - 1))

    level = one(*shards[0])
    for cut in shards[1:]:
        level = level * one(*cut)
    return level


def bell_draw(stream_key, extent, width, reach, cuts=(), held_as=jnp.bfloat16):
    array = jax.random.normal(stream_key, extent, jnp.float32) * width
    if len(cuts) > 0:
        array = block_scale(stream_key, extent, cuts, -0.22, 0.18) * array
    return jnp.clip(array, min=-reach, max=reach).astype(held_as)


def setup_inputs(seed: int = 0, part: int = 0) -> dict:
    key_list = jax.random.split(jax.random.key(seed), 8)
    part_splits = jax.random.split(jax.random.fold_in(key_list[7], part), 8)
    return {
        "tiles": bell_draw(part_splits[0], (TOKENS, D), 1.0, 6.0, ((0, 16),)),
        "tile_count": jax.random.randint(part_splits[1], (1,), TOKENS // 2, TOKENS + 1).astype(jnp.int32),
        "conv_weight": bell_draw(key_list[2], (25, D), 0.2, 3.0, (), jnp.float32),
        "conv_bias": bell_draw(key_list[3], (D,), 0.5, 3.0, (), jnp.float32),
        "ln_gain": jnp.clip(1.0 + 0.18 * jax.random.normal(key_list[4], (D,), jnp.float32), 0.1, 1.9),
        "w_qkv": draw_w_qkv(jax.random.fold_in(key_list[7], 71), part),
        "w_out": bell_draw(key_list[6], (D, D), D ** -0.5, 0.21875),
    }


EPS = 1e-05
NEG = -1e+30

def permitted_mask(query_index, key_index, dilation_step, active_count, head_total):
    shift_amounts = jnp.arange(head_total, dtype=jnp.int32) % dilation_step
    key_position = shift_amounts[:, None] + dilation_step * key_index[None, :]
    key_live = key_position < active_count
    return key_live[:, None, :] | (query_index[None, :, None] == key_index[None, None, :])

def attend_single_block(query_portion, key_portion, value_portion, allowed):
    score_scale = query_portion.shape[2] ** (-0.5)
    scores = jnp.einsum('qhd,khd->hqk', query_portion.astype(jnp.float32), key_portion.astype(jnp.float32)) * score_scale
    scores = jnp.where(allowed, scores, NEG)
    row_top = lax.optimization_barrier(jnp.max(scores, axis=2, keepdims=True))
    exp_terms = jnp.where(allowed, jnp.exp(scores - row_top), 0.0)
    denom_sum = lax.optimization_barrier(jnp.sum(exp_terms, axis=2))
    weights = exp_terms.astype(jnp.bfloat16)
    summed = jnp.einsum('hqk,khd->qhd', weights.astype(jnp.float32), value_portion.astype(jnp.float32))
    level_lse = jnp.transpose(row_top[:, :, 0] + jnp.log(denom_sum))
    return (summed / jnp.transpose(denom_sum)[:, :, None], level_lse)

def dilated_gather(source_rows, dilation_step):
    grouped_rows = source_rows.reshape(source_rows.shape[0] // dilation_step, dilation_step, source_rows.shape[1], source_rows.shape[2])
    return jnp.stack([grouped_rows[:, head_number % dilation_step, head_number] for head_number in range(source_rows.shape[1])], axis=1)

def scatter_back(sparse_output, sparse_logsumexp, dilation_step):
    heads_total = sparse_output.shape[1]
    match_flag = jnp.arange(dilation_step)[:, None] == (jnp.arange(heads_total) % dilation_step)[None, :]
    widened = sparse_output[:, None] * match_flag.astype(sparse_output.dtype)[None, :, :, None]
    lse_wide = jnp.where(match_flag[None], sparse_logsumexp[:, None, :], NEG)
    output_rows = sparse_output.shape[0] * dilation_step
    return (widened.reshape(output_rows, heads_total, sparse_output.shape[2]), lse_wide.reshape(output_rows, heads_total))

def merge_levels(level_outs, level_lses):
    top_all = jnp.maximum(jnp.maximum(level_lses[0], level_lses[1]), level_lses[2])
    factors = [jnp.exp(one_lse - top_all) for one_lse in level_lses]
    numer = factors[0][:, :, None] * level_outs[0] + factors[1][:, :, None] * level_outs[1] + factors[2][:, :, None] * level_outs[2]
    return numer / (factors[0] + factors[1] + factors[2])[:, :, None]

def attend_level(query_portion, key_portion, value_portion, dilation_step, active_count):
    segments = query_portion.shape[0] // TOK_DEV

    def per_segment(packed):
        seg_index, query_segment, key_segment, value_segment = packed
        sparse_index = seg_index * TOK_DEV + jnp.arange(TOK_DEV, dtype=jnp.int32)
        return attend_single_block(query_segment, key_segment, value_segment, permitted_mask(sparse_index, sparse_index, dilation_step, active_count, ATTENTION_HEADS))

    def shaped(source_rows):
        return source_rows.reshape(segments, TOK_DEV, ATTENTION_HEADS, source_rows.shape[2])
    result, lse_all = lax.map(per_segment, (jnp.arange(segments, dtype=jnp.int32), shaped(query_portion), shaped(key_portion), shaped(value_portion)))
    return (result.reshape(segments * TOK_DEV, ATTENTION_HEADS, query_portion.shape[2]), lse_all.reshape(segments * TOK_DEV, ATTENTION_HEADS))

def positional_sum(padded, column, conv_weight, halo_width, out_rows):
    summed = jnp.zeros((out_rows, padded.shape[1]), jnp.float32)
    for row_step in range(-2, 3):
        for col_step in range(-2, 3):
            start_row = halo_width + row_step * GW + col_step
            window = padded[start_row:start_row + out_rows]
            inside = ((column + col_step >= 0) & (column + col_step < GW)).astype(jnp.float32)
            summed = summed + window * (conv_weight[(row_step + 2) * 5 + col_step + 2][None, :] * inside[:, None])
    return summed

def normalize(mixed_in, ln_gain):
    row_mean = lax.optimization_barrier(jnp.mean(mixed_in, axis=1, keepdims=True))
    centred = mixed_in - row_mean
    row_var = lax.optimization_barrier(jnp.mean(centred * centred, axis=1, keepdims=True))
    return (centred * lax.rsqrt(row_var + EPS) * ln_gain).astype(jnp.bfloat16)

def reference(tiles, tile_count, conv_weight, conv_bias, ln_gain, w_qkv, w_out):
    active_count = tile_count[0]
    position = jnp.arange(TOKENS, dtype=jnp.int32)
    valid_row = (position < active_count).astype(jnp.float32)[:, None]
    masked = tiles * valid_row.astype(jnp.bfloat16)
    halo_width = 2 * GW + 2
    padded = jnp.pad(masked, ((halo_width, halo_width), (0, 0))).astype(jnp.float32)
    column = position % GW
    summed = positional_sum(padded, column, conv_weight, halo_width, TOKENS)
    mixed_in = (masked.astype(jnp.float32) + summed + conv_bias) * valid_row
    normed = normalize(mixed_in, ln_gain)
    projected = jnp.dot(normed, w_qkv, preferred_element_type=jnp.float32).astype(jnp.bfloat16)
    query_all = projected[:, :D].reshape(TOKENS, ATTENTION_HEADS, HD)
    key_all = projected[:, D:2 * D].reshape(TOKENS, ATTENTION_HEADS, HD)
    value_all = projected[:, 2 * D:].reshape(TOKENS, ATTENTION_HEADS, HD)
    near_out, near_lse = attend_level(query_all, key_all, value_all, 1, active_count)
    mid_sparse, mid_sparse_lse = attend_level(dilated_gather(query_all, MID_RATE), dilated_gather(key_all, MID_RATE), dilated_gather(value_all, MID_RATE), MID_RATE, active_count)
    far_sparse, far_sparse_lse = attend_level(dilated_gather(query_all, FAR_RATE), dilated_gather(key_all, FAR_RATE), dilated_gather(value_all, FAR_RATE), FAR_RATE, active_count)
    mid_out, mid_lse = scatter_back(mid_sparse, mid_sparse_lse, MID_RATE)
    far_out, far_lse = scatter_back(far_sparse, far_sparse_lse, FAR_RATE)
    heads_all = merge_levels((near_out, mid_out, far_out), (near_lse, mid_lse, far_lse))
    attended = (heads_all.reshape(TOKENS, D) * valid_row).astype(jnp.bfloat16)
    encoded = ((mixed_in + jnp.dot(attended, w_out, preferred_element_type=jnp.float32)) * valid_row).astype(jnp.bfloat16)
    return (attended, encoded)
```

```python
import functools

import jax
import jax.numpy as jnp
from jax import lax
from jax.experimental import pallas as pl
from jax.experimental.pallas import tpu as pltpu
from jax.sharding import PartitionSpec as P

ATTENTION_HEADS = 16
GW = 128
MID_RATE = 8


EPS = 1e-05
NEG = -1e30


def extended(block, sides, width):
    for axis, dim in sides:
        count = lax.axis_size(axis)
        forward = [(i, i + 1) for i in range(count - 1)]
        backward = [(target, source) for source, target in forward]
        low = lax.ppermute(
            lax.slice_in_dim(block, block.shape[dim] - width, None, axis=dim), axis, forward
        )
        high = lax.ppermute(lax.slice_in_dim(block, 0, width, axis=dim), axis, backward)
        block = jnp.concatenate([low, block, high], axis=dim)
    return block


def permitted_mask(query_index, key_index, dilation_step, active_count, head_total):
    shift_amounts = jnp.arange(head_total, dtype=jnp.int32) % dilation_step
    key_position = shift_amounts[:, None] + dilation_step * key_index[None, :]
    key_live = key_position < active_count
    return key_live[:, None, :] | (query_index[None, :, None] == key_index[None, None, :])


def attend_single_block(query_portion, key_portion, value_portion, allowed):
    score_scale = query_portion.shape[2] ** (-0.5)
    scores = (
        jnp.einsum("qhd,khd->hqk", query_portion, key_portion, preferred_element_type=jnp.float32)
        * score_scale
    )
    scores = jnp.where(allowed, scores, NEG)
    row_top = jnp.max(scores, axis=2, keepdims=True)
    exp_terms = jnp.where(allowed, jnp.exp(scores - row_top), 0.0)
    denom_sum = jnp.sum(exp_terms, axis=2)
    weights = exp_terms.astype(jnp.bfloat16)
    summed = jnp.einsum("hqk,khd->qhd", weights, value_portion, preferred_element_type=jnp.float32)
    level_lse = jnp.transpose(row_top[:, :, 0] + jnp.log(denom_sum))
    return (summed / jnp.transpose(denom_sum)[:, :, None], level_lse)


def offset_keep(dilation_step, model_width, head_size):
    step_index = jnp.arange(dilation_step, dtype=jnp.int32)[:, None]
    column_head = jnp.arange(model_width, dtype=jnp.int32)[None, :] // head_size
    return step_index == column_head % dilation_step


def dilated_rows(source_rows, dilation_step, head_size):
    model_width = source_rows.shape[1]
    grouped_rows = source_rows.reshape(
        source_rows.shape[0] // dilation_step, dilation_step, model_width
    )
    keep = offset_keep(dilation_step, model_width, head_size)
    return jnp.sum(jnp.where(keep[None], grouped_rows, jnp.zeros((), source_rows.dtype)), axis=1)


def scatter_back(sparse_output, sparse_logsumexp, dilation_step, head_size):
    sparse_rows, heads_total = sparse_logsumexp.shape
    model_width = heads_total * head_size
    flat_out = sparse_output.reshape(sparse_rows, model_width)
    keep = offset_keep(dilation_step, model_width, head_size)
    widened = jnp.where(keep[None], flat_out[:, None, :], 0.0)
    match_flag = (
        jnp.arange(dilation_step)[:, None] == (jnp.arange(heads_total) % dilation_step)[None, :]
    )
    lse_wide = jnp.where(match_flag[None], sparse_logsumexp[:, None, :], NEG)
    output_rows = sparse_rows * dilation_step
    return (
        widened.reshape(output_rows, heads_total, head_size),
        lse_wide.reshape(output_rows, heads_total),
    )


def merge_levels(level_outs, level_lses):
    top_all = jnp.maximum(jnp.maximum(level_lses[0], level_lses[1]), level_lses[2])
    factors = [jnp.exp(one_lse - top_all) for one_lse in level_lses]
    numer = (
        factors[0][:, :, None] * level_outs[0]
        + factors[1][:, :, None] * level_outs[1]
        + factors[2][:, :, None] * level_outs[2]
    )
    return numer / (factors[0] + factors[1] + factors[2])[:, :, None]


def positional_sum(padded, column, conv_weight, halo_width, out_rows):
    summed = jnp.zeros((out_rows, padded.shape[1]), jnp.float32)
    for row_step in range(-2, 3):
        for col_step in range(-2, 3):
            start_row = halo_width + row_step * GW + col_step
            window = padded[start_row : start_row + out_rows].astype(jnp.float32)
            inside = ((column + col_step >= 0) & (column + col_step < GW)).astype(jnp.float32)
            summed = summed + window * (
                conv_weight[(row_step + 2) * 5 + col_step + 2][None, :] * inside[:, None]
            )
    return summed


def normalize(mixed_in, ln_gain):
    row_mean = jnp.mean(mixed_in, axis=1, keepdims=True)
    centred = mixed_in - row_mean
    row_var = jnp.mean(centred * centred, axis=1, keepdims=True)
    return (centred * lax.rsqrt(row_var + EPS) * ln_gain).astype(jnp.bfloat16)


def shards(tiles, tile_count, conv_weight, conv_bias, ln_gain, w_qkv, w_out):
    local_rows = tiles.shape[0]
    model_width = tiles.shape[1]
    head_size = model_width // ATTENTION_HEADS
    devices = lax.axis_size("seq")
    dev_index = lax.axis_index("seq")
    active_count = tile_count[0]
    position = dev_index * local_rows + jnp.arange(local_rows, dtype=jnp.int32)
    valid_row = (position < active_count).astype(jnp.float32)[:, None]
    masked = tiles * valid_row.astype(jnp.bfloat16)
    halo_width = 2 * GW + 2
    padded = extended(masked, (("seq", 0),), halo_width)
    column = jnp.arange(local_rows, dtype=jnp.int32) % GW
    summed = positional_sum(padded, column, conv_weight, halo_width, local_rows)
    mixed_in = (masked.astype(jnp.float32) + summed + conv_bias) * valid_row
    normed = normalize(mixed_in, ln_gain)
    projected = jnp.dot(normed, w_qkv, preferred_element_type=jnp.float32).astype(jnp.bfloat16)
    query_flat = projected[:, :model_width]
    key_flat = projected[:, model_width : 2 * model_width]
    value_flat = projected[:, 2 * model_width :]

    def heads_of(flat_rows):
        return flat_rows.reshape(flat_rows.shape[0], ATTENTION_HEADS, head_size)

    near_out, near_lse = attend_single_block(
        heads_of(query_flat),
        heads_of(key_flat),
        heads_of(value_flat),
        permitted_mask(position, position, 1, active_count, ATTENTION_HEADS),
    )
    mid_rows = local_rows // MID_RATE
    mid_query = heads_of(dilated_rows(query_flat, MID_RATE, head_size))
    mid_kv = jnp.stack(
        [dilated_rows(key_flat, MID_RATE, head_size), dilated_rows(value_flat, MID_RATE, head_size)]
    )
    mid_query_idx = dev_index * mid_rows + jnp.arange(mid_rows, dtype=jnp.int32)
    group_base = dev_index // MID_RATE * local_rows
    far_rows = local_rows // devices
    far_query = heads_of(dilated_rows(query_flat, devices, head_size))
    far_kv = jnp.stack(
        [dilated_rows(key_flat, devices, head_size), dilated_rows(value_flat, devices, head_size)]
    )
    far_query_idx = dev_index * far_rows + jnp.arange(far_rows, dtype=jnp.int32)
    mid_all, far_all = (
        lax.all_gather(mid_kv, "seq", axis=1, tiled=True),
        lax.all_gather(far_kv, "seq", axis=1, tiled=True),
    )
    group_kv = lax.dynamic_slice_in_dim(mid_all, group_base, local_rows, 1)
    far_keys_idx = jnp.arange(local_rows, dtype=jnp.int32)
    far_sparse, far_sparse_lse = attend_single_block(
        far_query,
        heads_of(far_all[0]),
        heads_of(far_all[1]),
        permitted_mask(far_query_idx, far_keys_idx, devices, active_count, ATTENTION_HEADS),
    )
    group_idx = group_base + jnp.arange(local_rows, dtype=jnp.int32)
    mid_sparse, mid_sparse_lse = attend_single_block(
        mid_query,
        heads_of(group_kv[0]),
        heads_of(group_kv[1]),
        permitted_mask(mid_query_idx, group_idx, MID_RATE, active_count, ATTENTION_HEADS),
    )
    mid_out, mid_lse = scatter_back(mid_sparse, mid_sparse_lse, MID_RATE, head_size)
    far_out, far_lse = scatter_back(far_sparse, far_sparse_lse, devices, head_size)
    heads_all = merge_levels((near_out, mid_out, far_out), (near_lse, mid_lse, far_lse))
    attended = (heads_all.reshape(local_rows, model_width) * valid_row).astype(jnp.bfloat16)
    encoded = (
        (mixed_in + jnp.dot(attended, w_out, preferred_element_type=jnp.float32)) * valid_row
    ).astype(jnp.bfloat16)
    return (attended, encoded)


MESH = pl.DeviceIdType.MESH
LOG2E = 1.4426950408889634
LANES = 128
SLOT = 64
HALO = 2 * GW
LEAD = 8


def head_slots(model_width, head_size):
    packed = 8 * head_size
    slotted = 8 * SLOT
    source = lax.broadcasted_iota(jnp.int32, (packed, slotted), 0)
    target = lax.broadcasted_iota(jnp.int32, (packed, slotted), 1)
    inner = target % SLOT
    match = (inner < head_size) & (source == (target // SLOT) * head_size + inner)
    return jnp.where(match, 1.0, 0.0).astype(jnp.bfloat16)


def head_attention(query, key, value, half, bias, scale):
    lane = lax.broadcasted_iota(jnp.int32, query.shape, 1)
    own = jnp.where(lane // SLOT == half, query, jnp.zeros((), query.dtype))
    scores = lax.dot_general(
        own, key, (((1,), (1,)), ((), ())), preferred_element_type=jnp.float32
    )
    scores = scores * scale + bias
    top = jnp.max(scores, axis=1, keepdims=True)
    weights = jnp.exp2(scores - top).astype(jnp.bfloat16)
    return jnp.dot(weights, value, preferred_element_type=jnp.float32), top


def layer_kernel(
    devices, head_size,
    count_ref, tiles_ref, conv_w_ref, conv_b_ref, gain_ref, w_qkv_hbm, w_out_hbm,
    attended_ref, encoded_ref,
    w_qkv_ref, w_out_ref, halo_lo, halo_hi, ext, mixed, normed, qkv_wide, qkv, bias,
    near_r, near_m, mid_send, far_send, mid_recv, far_recv, mid_res, far_res,
    mid_back, far_back, slots_ref, att,
    w_sem, halo_send_sem, halo_recv_sem, mid_send_sem, mid_recv_sem, far_send_sem, far_recv_sem,
    mid_bs_sem, mid_br_sem, far_bs_sem, far_br_sem,
):
    rows, width = tiles_ref.shape
    me = lax.axis_index("seq")
    group = me // MID_RATE
    place = lax.rem(me, MID_RATE)
    mid_rows = rows // MID_RATE
    far_rows = rows // devices
    tiles_count = ATTENTION_HEADS // 2
    grid_rows = rows // GW
    scale = head_size ** (-0.5) * LOG2E
    count = count_ref[0]

    def weight_copy(i):
        source, target = ((w_qkv_hbm, w_qkv_ref), (w_out_hbm, w_out_ref))[i]
        return pltpu.make_async_copy(source, target, w_sem.at[i])

    weight_copy(0).start()
    weight_copy(1).start()

    barrier = pltpu.get_barrier_semaphore()

    def greet(k, carry):
        pl.semaphore_signal(
            barrier, inc=1, device_id={"seq": lax.rem(me + k, devices)}, device_id_type=MESH
        )
        return carry

    lax.fori_loop(1, devices, greet, 0)

    base = me * rows
    row_id = lax.broadcasted_iota(jnp.int32, (rows, 1), 0)
    valid = base + row_id < count

    def masked_of(block, first):
        at = first + lax.broadcasted_iota(jnp.int32, (block.shape[0], 1), 0)
        return jnp.where((at >= 0) & (at < count), block.astype(jnp.float32), 0.0)

    ext[0:LEAD, :] = jnp.zeros((LEAD, width), jnp.float32)
    ext[LEAD + 2 * HALO + rows :, :] = jnp.zeros((LEAD, width), jnp.float32)
    ext[LEAD : LEAD + HALO, :] = jnp.zeros((HALO, width), jnp.float32)
    ext[LEAD + HALO + rows : LEAD + 2 * HALO + rows, :] = jnp.zeros((HALO, width), jnp.float32)
    ext[LEAD + HALO : LEAD + HALO + rows, :] = masked_of(tiles_ref[...], base)

    pl.semaphore_wait(barrier, devices - 1)

    def up_copy():
        return pltpu.make_async_remote_copy(
            src_ref=tiles_ref.at[pl.ds(rows - HALO, HALO), :], dst_ref=halo_lo,
            send_sem=halo_send_sem.at[0], recv_sem=halo_recv_sem.at[0],
            device_id={"seq": me + 1}, device_id_type=MESH,
        )

    def down_copy():
        return pltpu.make_async_remote_copy(
            src_ref=tiles_ref.at[pl.ds(0, HALO), :], dst_ref=halo_hi,
            send_sem=halo_send_sem.at[1], recv_sem=halo_recv_sem.at[1],
            device_id={"seq": me - 1}, device_id_type=MESH,
        )

    @pl.when(me < devices - 1)
    def _():
        up_copy().start()

    @pl.when(me > 0)
    def _():
        down_copy().start()

    slots_ref[...] = head_slots(width, head_size)
    key_at = lax.broadcasted_iota(jnp.int32, (rows, rows), 1)
    query_at = lax.broadcasted_iota(jnp.int32, (rows, rows), 0)
    bias[...] = jnp.where((base + key_at < count) | (query_at == key_at), 0.0, NEG)

    column = lax.broadcasted_iota(jnp.int32, (GW, LANES), 0)

    def conv_rows(r, row_steps, lanes, total):
        for b in range(-2, 3):
            part = None
            for a in row_steps:
                start = LEAD + HALO + (r + a) * GW + b
                term = ext[start : start + GW, lanes] * conv_w_ref[
                    (a + 2) * 5 + b + 2 : (a + 2) * 5 + b + 3, lanes
                ]
                part = term if part is None else part + term
            if b != 0:
                part = jnp.where((column + b >= 0) & (column + b < GW), part, 0.0)
            total = total + part
        return total

    def inner_conv(t, carry):
        lanes = pl.ds(pl.multiple_of(t * LANES, LANES), LANES)
        for r in range(grid_rows):
            here = slice(r * GW, (r + 1) * GW)
            start = LEAD + HALO + r * GW
            total = ext[start : start + GW, lanes] + conv_b_ref[:, lanes]
            steps = [a for a in range(-2, 3) if 0 <= r + a < grid_rows]
            mixed[here, lanes] = conv_rows(r, steps, lanes, total)
        return carry

    lax.fori_loop(0, width // LANES, inner_conv, 0)

    @pl.when(me > 0)
    def _():
        up_copy().wait_recv()
        ext[LEAD : LEAD + HALO, :] = masked_of(halo_lo[...], base - HALO)

    @pl.when(me < devices - 1)
    def _():
        down_copy().wait_recv()
        ext[LEAD + HALO + rows : LEAD + 2 * HALO + rows, :] = masked_of(halo_hi[...], base + rows)

    def outer_conv(t, carry):
        lanes = pl.ds(pl.multiple_of(t * LANES, LANES), LANES)
        for r in range(grid_rows):
            here = slice(r * GW, (r + 1) * GW)
            steps = [a for a in range(-2, 3) if not 0 <= r + a < grid_rows]
            mixed[here, lanes] = jnp.where(
                base + r * GW + column < count,
                conv_rows(r, steps, lanes, mixed[here, lanes]) if steps else mixed[here, lanes],
                0.0,
            )
        return carry

    lax.fori_loop(0, width // LANES, outer_conv, 0)

    def norm_rows(i, carry):
        here = pl.ds(pl.multiple_of(i * GW, GW), GW)
        x = mixed[here, :]
        centred = x - jnp.mean(x, axis=1, keepdims=True)
        var = jnp.mean(centred * centred, axis=1, keepdims=True)
        normed[here, :] = (centred * lax.rsqrt(var + EPS) * gain_ref[...]).astype(jnp.bfloat16)
        return carry

    lax.fori_loop(0, grid_rows, norm_rows, 0)

    lane = lax.broadcasted_iota(jnp.int32, (1, LANES), 1)
    spare = lane % SLOT >= head_size
    low = lane < SLOT
    weight_copy(0).wait()
    block = 8 * head_size
    per_block = 8 * SLOT // LANES

    for b in range(3 * width // block):
        some = jnp.dot(
            normed[...], w_qkv_ref[:, b * block : (b + 1) * block],
            preferred_element_type=jnp.float32,
        ).astype(jnp.bfloat16)
        spread = jnp.dot(some, slots_ref[...], preferred_element_type=jnp.float32)
        for i in range(per_block):
            tile = spread[:, i * LANES : (i + 1) * LANES]
            if b * block >= 2 * width:
                tile = jnp.where(spare, 1.0, tile)
            qkv_wide[b * per_block + i] = tile
            qkv[b * per_block + i] = tile.astype(jnp.bfloat16)

    for g in range(tiles_count):
        for c in range(3):
            from_tile = c * tiles_count + g

            def picked(stride, amount):
                one = qkv_wide[from_tile, pl.ds((2 * g) % stride, amount, stride=stride), :]
                two = qkv_wide[from_tile, pl.ds((2 * g + 1) % stride, amount, stride=stride), :]
                return jnp.where(low, one, two).astype(jnp.bfloat16)

            mid_send[g, c] = picked(MID_RATE, mid_rows)
            far_send[g, c] = picked(devices, far_rows)

    def mid_at(index):
        return pl.ds(pl.multiple_of(index * mid_rows, mid_rows), mid_rows)

    def far_at(index):
        return pl.ds(pl.multiple_of(index * far_rows, far_rows), far_rows)

    def mid_out_copy(k, origin):
        to = lax.rem(place + k, MID_RATE)
        return pltpu.make_async_remote_copy(
            src_ref=mid_send.at[to], dst_ref=mid_recv.at[:, mid_at(origin), :],
            send_sem=mid_send_sem.at[k], recv_sem=mid_recv_sem.at[k],
            device_id={"seq": group * MID_RATE + to}, device_id_type=MESH,
        )

    def far_out_copy(k, origin):
        to = lax.rem(me + k, devices)
        return pltpu.make_async_remote_copy(
            src_ref=far_send.at[to // 2], dst_ref=far_recv.at[:, far_at(origin), :],
            send_sem=far_send_sem.at[k], recv_sem=far_recv_sem.at[k],
            device_id={"seq": to}, device_id_type=MESH,
        )

    def mid_back_copy(k, origin):
        to = lax.rem(place + k, MID_RATE)
        return pltpu.make_async_remote_copy(
            src_ref=mid_res.at[mid_at(to), :], dst_ref=mid_back.at[origin],
            send_sem=mid_bs_sem.at[k], recv_sem=mid_br_sem.at[k],
            device_id={"seq": group * MID_RATE + to}, device_id_type=MESH,
        )

    def far_back_copy(k, origin):
        to = lax.rem(me + k, devices)
        return pltpu.make_async_remote_copy(
            src_ref=far_res.at[far_at(to), :], dst_ref=far_back.at[origin],
            send_sem=far_bs_sem.at[k], recv_sem=far_br_sem.at[k],
            device_id={"seq": to}, device_id_type=MESH,
        )

    def start_all(copy, mine, size):
        def one(k, carry):
            copy(k, mine).start()
            return carry

        lax.fori_loop(1, size, one, 0)

    def receive_all(copy, mine, size):
        def one(k, carry):
            copy(k, lax.rem(mine + size - k, size)).wait_recv()
            return carry

        lax.fori_loop(1, size, one, 0)

    def sent_all(copy, mine, size):
        def one(k, carry):
            copy(k, mine).wait_send()
            return carry

        lax.fori_loop(1, size, one, 0)

    start_all(far_out_copy, me, devices)
    start_all(mid_out_copy, place, MID_RATE)
    mid_recv[:, mid_at(place), :] = mid_send[place]
    far_recv[:, far_at(me), :] = far_send[me // 2]

    def near_pair(g, carry):
        query, key, value = qkv[g], qkv[tiles_count + g], qkv[2 * tiles_count + g]
        one, one_top = head_attention(query, key, value, 0, bias[...], scale)
        two, two_top = head_attention(query, key, value, 1, bias[...], scale)
        near_r[g] = jnp.where(low, one, two)
        near_m[g] = jnp.where(low, one_top, two_top)
        return carry

    before = tiles_count - 2
    lax.fori_loop(0, before, near_pair, 0)

    def packed(result, top):
        return jnp.where(lane % SLOT >= SLOT - 8, top, result)

    def level_bias(offset, step, first):
        at = offset + step * (first + key_at)
        return jnp.where((at < count) | (query_at == key_at), 0.0, NEG)

    receive_all(mid_out_copy, place, MID_RATE)
    halves = []
    for half in range(2):
        offset = lax.rem(2 * place + half, MID_RATE)
        halves.append(
            packed(*head_attention(
                mid_recv[0], mid_recv[1], mid_recv[2], half,
                level_bias(offset, MID_RATE, group * rows), scale,
            ))
        )
    mid_res[...] = jnp.where(low, halves[0], halves[1])
    start_all(mid_back_copy, place, MID_RATE)
    mid_back[place] = mid_res[mid_at(place), :]

    receive_all(far_out_copy, me, devices)
    far_res[...] = packed(*head_attention(
        far_recv[0], far_recv[1], far_recv[2], lax.rem(me, 2),
        level_bias(me, devices, 0), scale,
    ))
    start_all(far_back_copy, me, devices)
    far_back[me] = far_res[far_at(me), :]

    lax.fori_loop(before, tiles_count, near_pair, 0)

    receive_all(mid_back_copy, place, MID_RATE)
    receive_all(far_back_copy, me, devices)

    def sum_of(tile):
        return jnp.where(
            low, tile[:, head_size : head_size + 1], tile[:, SLOT + head_size : SLOT + head_size + 1]
        )

    def top_of(tile):
        return jnp.where(low, tile[:, SLOT - 1 : SLOT], tile[:, 2 * SLOT - 1 : 2 * SLOT])

    def widen(tile, step):
        return jnp.broadcast_to(
            tile[:, None, :], (tile.shape[0], step, LANES)
        ).reshape(rows, LANES)

    def merge_pair(g, carry):
        head = 2 * g + jnp.where(low, 0, 1)
        far = jnp.where(low, far_back[2 * g], far_back[2 * g + 1])
        mid = mid_back[g]
        mid_on = row_id % MID_RATE == head % MID_RATE
        far_on = row_id % devices == head % devices
        near = near_r[g]
        tops = (
            near_m[g],
            jnp.where(mid_on, widen(top_of(mid), MID_RATE), NEG),
            jnp.where(far_on, widen(top_of(far), devices), NEG),
        )
        top = jnp.maximum(jnp.maximum(tops[0], tops[1]), tops[2])
        factors = [jnp.exp2(one - top) for one in tops]
        numer = (
            factors[0] * near
            + factors[1] * widen(mid, MID_RATE)
            + factors[2] * widen(far, devices)
        )
        denom = (
            factors[0] * sum_of(near)
            + factors[1] * widen(sum_of(mid), MID_RATE)
            + factors[2] * widen(sum_of(far), devices)
        )
        att[g] = jnp.where(valid & jnp.logical_not(spare), numer / denom, 0.0).astype(jnp.bfloat16)
        return carry

    lax.fori_loop(0, tiles_count, merge_pair, 0)

    weight_copy(1).wait()
    for i in range(width // block):
        some = jnp.concatenate([att[i * per_block + j] for j in range(per_block)], axis=1)
        attended_ref[:, i * block : (i + 1) * block] = lax.dot_general(
            some, slots_ref[...], (((1,), (1,)), ((), ())), preferred_element_type=jnp.float32
        ).astype(jnp.bfloat16)
    for i in range(width // block):
        here = slice(i * block, (i + 1) * block)
        out = mixed[:, here] + jnp.dot(
            attended_ref[...], w_out_ref[:, here], preferred_element_type=jnp.float32
        )
        encoded_ref[:, here] = jnp.where(valid, out, 0.0).astype(jnp.bfloat16)

    @pl.when(me < devices - 1)
    def _():
        up_copy().wait_send()

    @pl.when(me > 0)
    def _():
        down_copy().wait_send()

    sent_all(mid_out_copy, place, MID_RATE)
    sent_all(far_out_copy, me, devices)
    sent_all(mid_back_copy, place, MID_RATE)
    sent_all(far_back_copy, me, devices)


def fused(tiles, tile_count, conv_weight, conv_bias, ln_gain, w_qkv, w_out):
    rows, width = tiles.shape
    devices = lax.axis_size("seq")
    head_size = width // ATTENTION_HEADS
    pairs = ATTENTION_HEADS // 2
    mid_rows, far_rows = rows // MID_RATE, rows // devices
    bf16, f32 = jnp.bfloat16, jnp.float32
    vmem = pl.BlockSpec(memory_space=pltpu.VMEM)
    anyspace = pl.BlockSpec(memory_space=pl.ANY)
    dma = pltpu.SemaphoreType.DMA
    return pl.pallas_call(
        functools.partial(layer_kernel, devices, head_size),
        out_shape=[jax.ShapeDtypeStruct((rows, width), bf16)] * 2,
        in_specs=[pl.BlockSpec(memory_space=pltpu.SMEM)] + [vmem] * 4 + [anyspace] * 2,
        out_specs=[vmem] * 2,
        scratch_shapes=[
            pltpu.VMEM(w_qkv.shape, bf16),
            pltpu.VMEM(w_out.shape, bf16),
            pltpu.VMEM((HALO, width), bf16),
            pltpu.VMEM((HALO, width), bf16),
            pltpu.VMEM((rows + 2 * HALO + 2 * LEAD, width), f32),
            pltpu.VMEM((rows, width), f32),
            pltpu.VMEM((rows, width), bf16),
            pltpu.VMEM((3 * pairs, rows, LANES), f32),
            pltpu.VMEM((3 * pairs, rows, LANES), bf16),
            pltpu.VMEM((rows, rows), f32),
            pltpu.VMEM((pairs, rows, LANES), f32),
            pltpu.VMEM((pairs, rows, LANES), f32),
            pltpu.VMEM((pairs, 3, mid_rows, LANES), bf16),
            pltpu.VMEM((pairs, 3, far_rows, LANES), bf16),
            pltpu.VMEM((3, rows, LANES), bf16),
            pltpu.VMEM((3, rows, LANES), bf16),
            pltpu.VMEM((rows, LANES), f32),
            pltpu.VMEM((rows, LANES), f32),
            pltpu.VMEM((pairs, mid_rows, LANES), f32),
            pltpu.VMEM((ATTENTION_HEADS, far_rows, LANES), f32),
            pltpu.VMEM((8 * head_size, 8 * SLOT), bf16),
            pltpu.VMEM((pairs, rows, LANES), bf16),
            dma((2,)), dma((2,)), dma((2,)),
            dma((MID_RATE,)), dma((MID_RATE,)), dma((devices,)), dma((devices,)),
            dma((MID_RATE,)), dma((MID_RATE,)), dma((devices,)), dma((devices,)),
        ],
        compiler_params=pltpu.CompilerParams(
            collective_id=0, has_side_effects=True, vmem_limit_bytes=50 * 1024 * 1024
        ),
    )(tile_count, tiles, conv_weight, conv_bias[None], ln_gain[None], w_qkv, w_out)


def solution(mesh):
    placed = (P(("slides", "seq"), None), P("slides"), P(), P(), P(), P(), P())
    body = fused if mesh.shape["seq"] == ATTENTION_HEADS else shards
    return jax.shard_map(
        body,
        mesh=mesh,
        in_specs=placed,
        out_specs=(P(("slides", "seq"), None), P(("slides", "seq"), None)),
        check_vma=False,
    )
```

```python
import functools

import jax
import jax.numpy as jnp
from jax import lax
from jax.experimental import pallas as pl
from jax.experimental.pallas import tpu as pltpu
from jax.sharding import PartitionSpec as P

ATTENTION_HEADS = 16
GW = 128
MID_RATE = 8


EPS = 1e-05
NEG = -1e30


def extended(block, sides, width):
    for axis, dim in sides:
        count = lax.axis_size(axis)
        forward = [(i, i + 1) for i in range(count - 1)]
        backward = [(target, source) for source, target in forward]
        low = lax.ppermute(
            lax.slice_in_dim(block, block.shape[dim] - width, None, axis=dim), axis, forward
        )
        high = lax.ppermute(lax.slice_in_dim(block, 0, width, axis=dim), axis, backward)
        block = jnp.concatenate([low, block, high], axis=dim)
    return block


def permitted_mask(query_index, key_index, dilation_step, active_count, head_total):
    shift_amounts = jnp.arange(head_total, dtype=jnp.int32) % dilation_step
    key_position = shift_amounts[:, None] + dilation_step * key_index[None, :]
    key_live = key_position < active_count
    return key_live[:, None, :] | (query_index[None, :, None] == key_index[None, None, :])


def attend_single_block(query_portion, key_portion, value_portion, allowed):
    score_scale = query_portion.shape[2] ** (-0.5)
    scores = (
        jnp.einsum("qhd,khd->hqk", query_portion, key_portion, preferred_element_type=jnp.float32)
        * score_scale
    )
    scores = jnp.where(allowed, scores, NEG)
    row_top = jnp.max(scores, axis=2, keepdims=True)
    exp_terms = jnp.where(allowed, jnp.exp(scores - row_top), 0.0)
    denom_sum = jnp.sum(exp_terms, axis=2)
    weights = exp_terms.astype(jnp.bfloat16)
    summed = jnp.einsum("hqk,khd->qhd", weights, value_portion, preferred_element_type=jnp.float32)
    level_lse = jnp.transpose(row_top[:, :, 0] + jnp.log(denom_sum))
    return (summed / jnp.transpose(denom_sum)[:, :, None], level_lse)


def offset_keep(dilation_step, model_width, head_size):
    step_index = jnp.arange(dilation_step, dtype=jnp.int32)[:, None]
    column_head = jnp.arange(model_width, dtype=jnp.int32)[None, :] // head_size
    return step_index == column_head % dilation_step


def dilated_rows(source_rows, dilation_step, head_size):
    model_width = source_rows.shape[1]
    grouped_rows = source_rows.reshape(
        source_rows.shape[0] // dilation_step, dilation_step, model_width
    )
    keep = offset_keep(dilation_step, model_width, head_size)
    return jnp.sum(jnp.where(keep[None], grouped_rows, jnp.zeros((), source_rows.dtype)), axis=1)


def scatter_back(sparse_output, sparse_logsumexp, dilation_step, head_size):
    sparse_rows, heads_total = sparse_logsumexp.shape
    model_width = heads_total * head_size
    flat_out = sparse_output.reshape(sparse_rows, model_width)
    keep = offset_keep(dilation_step, model_width, head_size)
    widened = jnp.where(keep[None], flat_out[:, None, :], 0.0)
    match_flag = (
        jnp.arange(dilation_step)[:, None] == (jnp.arange(heads_total) % dilation_step)[None, :]
    )
    lse_wide = jnp.where(match_flag[None], sparse_logsumexp[:, None, :], NEG)
    output_rows = sparse_rows * dilation_step
    return (
        widened.reshape(output_rows, heads_total, head_size),
        lse_wide.reshape(output_rows, heads_total),
    )


def merge_levels(level_outs, level_lses):
    top_all = jnp.maximum(jnp.maximum(level_lses[0], level_lses[1]), level_lses[2])
    factors = [jnp.exp(one_lse - top_all) for one_lse in level_lses]
    numer = (
        factors[0][:, :, None] * level_outs[0]
        + factors[1][:, :, None] * level_outs[1]
        + factors[2][:, :, None] * level_outs[2]
    )
    return numer / (factors[0] + factors[1] + factors[2])[:, :, None]


def positional_sum(padded, column, conv_weight, halo_width, out_rows):
    summed = jnp.zeros((out_rows, padded.shape[1]), jnp.float32)
    for row_step in range(-2, 3):
        for col_step in range(-2, 3):
            start_row = halo_width + row_step * GW + col_step
            window = padded[start_row : start_row + out_rows].astype(jnp.float32)
            inside = ((column + col_step >= 0) & (column + col_step < GW)).astype(jnp.float32)
            summed = summed + window * (
                conv_weight[(row_step + 2) * 5 + col_step + 2][None, :] * inside[:, None]
            )
    return summed


def normalize(mixed_in, ln_gain):
    row_mean = jnp.mean(mixed_in, axis=1, keepdims=True)
    centred = mixed_in - row_mean
    row_var = jnp.mean(centred * centred, axis=1, keepdims=True)
    return (centred * lax.rsqrt(row_var + EPS) * ln_gain).astype(jnp.bfloat16)


def shards(tiles, tile_count, conv_weight, conv_bias, ln_gain, w_qkv, w_out):
    local_rows = tiles.shape[0]
    model_width = tiles.shape[1]
    head_size = model_width // ATTENTION_HEADS
    devices = lax.axis_size("seq")
    dev_index = lax.axis_index("seq")
    active_count = tile_count[0]
    position = dev_index * local_rows + jnp.arange(local_rows, dtype=jnp.int32)
    valid_row = (position < active_count).astype(jnp.float32)[:, None]
    masked = tiles * valid_row.astype(jnp.bfloat16)
    halo_width = 2 * GW + 2
    padded = extended(masked, (("seq", 0),), halo_width)
    column = jnp.arange(local_rows, dtype=jnp.int32) % GW
    summed = positional_sum(padded, column, conv_weight, halo_width, local_rows)
    mixed_in = (masked.astype(jnp.float32) + summed + conv_bias) * valid_row
    normed = normalize(mixed_in, ln_gain)
    projected = jnp.dot(normed, w_qkv, preferred_element_type=jnp.float32).astype(jnp.bfloat16)
    query_flat = projected[:, :model_width]
    key_flat = projected[:, model_width : 2 * model_width]
    value_flat = projected[:, 2 * model_width :]

    def heads_of(flat_rows):
        return flat_rows.reshape(flat_rows.shape[0], ATTENTION_HEADS, head_size)

    near_out, near_lse = attend_single_block(
        heads_of(query_flat),
        heads_of(key_flat),
        heads_of(value_flat),
        permitted_mask(position, position, 1, active_count, ATTENTION_HEADS),
    )
    mid_rows = local_rows // MID_RATE
    mid_query = heads_of(dilated_rows(query_flat, MID_RATE, head_size))
    mid_kv = jnp.stack(
        [dilated_rows(key_flat, MID_RATE, head_size), dilated_rows(value_flat, MID_RATE, head_size)]
    )
    mid_query_idx = dev_index * mid_rows + jnp.arange(mid_rows, dtype=jnp.int32)
    group_base = dev_index // MID_RATE * local_rows
    far_rows = local_rows // devices
    far_query = heads_of(dilated_rows(query_flat, devices, head_size))
    far_kv = jnp.stack(
        [dilated_rows(key_flat, devices, head_size), dilated_rows(value_flat, devices, head_size)]
    )
    far_query_idx = dev_index * far_rows + jnp.arange(far_rows, dtype=jnp.int32)
    mid_all, far_all = (
        lax.all_gather(mid_kv, "seq", axis=1, tiled=True),
        lax.all_gather(far_kv, "seq", axis=1, tiled=True),
    )
    group_kv = lax.dynamic_slice_in_dim(mid_all, group_base, local_rows, 1)
    far_keys_idx = jnp.arange(local_rows, dtype=jnp.int32)
    far_sparse, far_sparse_lse = attend_single_block(
        far_query,
        heads_of(far_all[0]),
        heads_of(far_all[1]),
        permitted_mask(far_query_idx, far_keys_idx, devices, active_count, ATTENTION_HEADS),
    )
    group_idx = group_base + jnp.arange(local_rows, dtype=jnp.int32)
    mid_sparse, mid_sparse_lse = attend_single_block(
        mid_query,
        heads_of(group_kv[0]),
        heads_of(group_kv[1]),
        permitted_mask(mid_query_idx, group_idx, MID_RATE, active_count, ATTENTION_HEADS),
    )
    mid_out, mid_lse = scatter_back(mid_sparse, mid_sparse_lse, MID_RATE, head_size)
    far_out, far_lse = scatter_back(far_sparse, far_sparse_lse, devices, head_size)
    heads_all = merge_levels((near_out, mid_out, far_out), (near_lse, mid_lse, far_lse))
    attended = (heads_all.reshape(local_rows, model_width) * valid_row).astype(jnp.bfloat16)
    encoded = (
        (mixed_in + jnp.dot(attended, w_out, preferred_element_type=jnp.float32)) * valid_row
    ).astype(jnp.bfloat16)
    return (attended, encoded)


MESH = pl.DeviceIdType.MESH
LOG2E = 1.4426950408889634
LANES = 128
SLOT = 64
HALO = 2 * GW
LEAD = 8


def head_slots(model_width, head_size):
    packed = 8 * head_size
    slotted = 8 * SLOT
    source = lax.broadcasted_iota(jnp.int32, (packed, slotted), 0)
    target = lax.broadcasted_iota(jnp.int32, (packed, slotted), 1)
    inner = target % SLOT
    match = (inner < head_size) & (source == (target // SLOT) * head_size + inner)
    return jnp.where(match, 1.0, 0.0).astype(jnp.bfloat16)


def head_attention(query, key, value, half, bias, scale):
    lane = lax.broadcasted_iota(jnp.int32, query.shape, 1)
    own = jnp.where(lane // SLOT == half, query, jnp.zeros((), query.dtype))
    scores = lax.dot_general(
        own, key, (((1,), (1,)), ((), ())), preferred_element_type=jnp.float32
    )
    scores = scores * scale + bias
    top = jnp.max(scores, axis=1, keepdims=True)
    weights = jnp.exp2(scores - top).astype(jnp.bfloat16)
    return jnp.dot(weights, value, preferred_element_type=jnp.float32), top


def layer_kernel(
    devices, head_size,
    count_ref, tiles_hbm, conv_w_hbm, conv_b_hbm, gain_hbm, w_qkv_hbm, w_out_hbm,
    attended_ref, encoded_ref,
    tiles_ref, conv_w_ref, conv_b_ref, gain_ref, w_qkv_ref, w_out_ref, halo_lo, halo_hi, ext, mixed, normed, qkv_wide, qkv, bias,
    near_r, near_m, mid_send, far_send, mid_recv, far_recv, mid_res, far_res,
    mid_back, far_back, slots_ref, att,
    w_sem, halo_send_sem, halo_recv_sem, mid_send_sem, mid_recv_sem, far_send_sem, far_recv_sem,
    mid_bs_sem, mid_br_sem, far_bs_sem, far_br_sem,
):
    rows, width = tiles_ref.shape
    me = lax.axis_index("seq")
    group = me // MID_RATE
    place = lax.rem(me, MID_RATE)
    mid_rows = rows // MID_RATE
    far_rows = rows // devices
    tiles_count = ATTENTION_HEADS // 2
    grid_rows = rows // GW
    scale = head_size ** (-0.5) * LOG2E
    count = count_ref[0]

    def weight_copy(i):
        source, target = (
            (w_qkv_hbm, w_qkv_ref), (w_out_hbm, w_out_ref), (tiles_hbm, tiles_ref),
            (conv_w_hbm, conv_w_ref), (conv_b_hbm, conv_b_ref), (gain_hbm, gain_ref),
        )[i]
        return pltpu.make_async_copy(source, target, w_sem.at[i])

    for i in (2, 3, 4, 5, 0, 1):
        weight_copy(i).start()

    barrier = pltpu.get_barrier_semaphore()

    def greet(k, carry):
        pl.semaphore_signal(
            barrier, inc=1, device_id={"seq": lax.rem(me + k, devices)}, device_id_type=MESH
        )
        return carry

    lax.fori_loop(1, devices, greet, 0)

    base = me * rows
    row_id = lax.broadcasted_iota(jnp.int32, (rows, 1), 0)
    valid = base + row_id < count

    def masked_of(block, first):
        at = first + lax.broadcasted_iota(jnp.int32, (block.shape[0], 1), 0)
        return jnp.where((at >= 0) & (at < count), block.astype(jnp.float32), 0.0)

    ext[0:LEAD, :] = jnp.zeros((LEAD, width), jnp.float32)
    ext[LEAD + 2 * HALO + rows :, :] = jnp.zeros((LEAD, width), jnp.float32)
    ext[LEAD : LEAD + HALO, :] = jnp.zeros((HALO, width), jnp.float32)
    ext[LEAD + HALO + rows : LEAD + 2 * HALO + rows, :] = jnp.zeros((HALO, width), jnp.float32)
    pl.semaphore_wait(barrier, devices - 1)

    def up_copy():
        return pltpu.make_async_remote_copy(
            src_ref=tiles_hbm.at[pl.ds(rows - HALO, HALO), :], dst_ref=halo_lo,
            send_sem=halo_send_sem.at[0], recv_sem=halo_recv_sem.at[0],
            device_id={"seq": me + 1}, device_id_type=MESH,
        )

    def down_copy():
        return pltpu.make_async_remote_copy(
            src_ref=tiles_hbm.at[pl.ds(0, HALO), :], dst_ref=halo_hi,
            send_sem=halo_send_sem.at[1], recv_sem=halo_recv_sem.at[1],
            device_id={"seq": me - 1}, device_id_type=MESH,
        )

    @pl.when(me < devices - 1)
    def _():
        up_copy().start()

    @pl.when(me > 0)
    def _():
        down_copy().start()

    for i in (2, 3, 4, 5):
        weight_copy(i).wait()
    ext[LEAD + HALO : LEAD + HALO + rows, :] = masked_of(tiles_ref[...], base)
    slots_ref[...] = head_slots(width, head_size)
    key_at = lax.broadcasted_iota(jnp.int32, (rows, rows), 1)
    query_at = lax.broadcasted_iota(jnp.int32, (rows, rows), 0)
    bias[...] = jnp.where((base + key_at < count) | (query_at == key_at), 0.0, NEG)

    column = lax.broadcasted_iota(jnp.int32, (GW, LANES), 0)

    def conv_rows(r, row_steps, lanes, total):
        for b in range(-2, 3):
            part = None
            for a in row_steps:
                start = LEAD + HALO + (r + a) * GW + b
                term = ext[start : start + GW, lanes] * conv_w_ref[
                    (a + 2) * 5 + b + 2 : (a + 2) * 5 + b + 3, lanes
                ]
                part = term if part is None else part + term
            if b != 0:
                part = jnp.where((column + b >= 0) & (column + b < GW), part, 0.0)
            total = total + part
        return total

    def inner_conv(t, carry):
        lanes = pl.ds(pl.multiple_of(t * LANES, LANES), LANES)
        for r in range(grid_rows):
            here = slice(r * GW, (r + 1) * GW)
            start = LEAD + HALO + r * GW
            total = ext[start : start + GW, lanes] + conv_b_ref[lanes][None]
            steps = [a for a in range(-2, 3) if 0 <= r + a < grid_rows]
            mixed[here, lanes] = conv_rows(r, steps, lanes, total)
        return carry

    lax.fori_loop(0, width // LANES, inner_conv, 0)

    @pl.when(me > 0)
    def _():
        up_copy().wait_recv()
        ext[LEAD : LEAD + HALO, :] = masked_of(halo_lo[...], base - HALO)

    @pl.when(me < devices - 1)
    def _():
        down_copy().wait_recv()
        ext[LEAD + HALO + rows : LEAD + 2 * HALO + rows, :] = masked_of(halo_hi[...], base + rows)

    def outer_conv(t, carry):
        lanes = pl.ds(pl.multiple_of(t * LANES, LANES), LANES)
        for r in range(grid_rows):
            here = slice(r * GW, (r + 1) * GW)
            steps = [a for a in range(-2, 3) if not 0 <= r + a < grid_rows]
            mixed[here, lanes] = jnp.where(
                base + r * GW + column < count,
                conv_rows(r, steps, lanes, mixed[here, lanes]) if steps else mixed[here, lanes],
                0.0,
            )
        return carry

    lax.fori_loop(0, width // LANES, outer_conv, 0)

    def norm_rows(i, carry):
        here = pl.ds(pl.multiple_of(i * GW, GW), GW)
        x = mixed[here, :]
        centred = x - jnp.mean(x, axis=1, keepdims=True)
        var = jnp.mean(centred * centred, axis=1, keepdims=True)
        normed[here, :] = (centred * lax.rsqrt(var + EPS) * gain_ref[...][None]).astype(jnp.bfloat16)
        return carry

    lax.fori_loop(0, grid_rows, norm_rows, 0)

    lane = lax.broadcasted_iota(jnp.int32, (1, LANES), 1)
    spare = lane % SLOT >= head_size
    low = lane < SLOT
    weight_copy(0).wait()
    block = 8 * head_size
    per_block = 8 * SLOT // LANES

    for b in range(3 * width // block):
        some = jnp.dot(
            normed[...], w_qkv_ref[:, b * block : (b + 1) * block],
            preferred_element_type=jnp.float32,
        ).astype(jnp.bfloat16)
        spread = jnp.dot(some, slots_ref[...], preferred_element_type=jnp.float32)
        for i in range(per_block):
            tile = spread[:, i * LANES : (i + 1) * LANES]
            if b * block >= 2 * width:
                tile = jnp.where(spare, 1.0, tile)
            qkv_wide[b * per_block + i] = tile
            qkv[b * per_block + i] = tile.astype(jnp.bfloat16)

    fold = far_rows // 2

    def swapped(x):
        return pltpu.roll(x, SLOT, x.ndim - 1)

    for g in range(tiles_count):
        for c in range(3):
            from_tile = c * tiles_count + g

            one = qkv_wide[from_tile, pl.ds((2 * g) % MID_RATE, mid_rows, stride=MID_RATE), :]
            two = qkv_wide[from_tile, pl.ds((2 * g + 1) % MID_RATE, mid_rows, stride=MID_RATE), :]
            mid_send[g, c] = jnp.where(low, one, two).astype(jnp.bfloat16)
        for half in range(2):
            query, key, value = (
                qkv_wide[c * tiles_count + g, pl.ds(2 * g + half, far_rows, stride=devices), :]
                for c in range(3)
            )
            if half == 0:
                key, last = swapped(key), swapped(value[fold:])
                first = value[:fold]
            else:
                query, first = swapped(query), swapped(value[:fold])
                last = value[fold:]
            far_send[2 * g + half, :far_rows] = jnp.where(low, query, key).astype(jnp.bfloat16)
            far_send[2 * g + half, far_rows:] = jnp.where(low, first, last).astype(jnp.bfloat16)

    def mid_at(index):
        return pl.ds(pl.multiple_of(index * mid_rows, mid_rows), mid_rows)

    def mid_out_copy(k, origin):
        to = lax.rem(place + k, MID_RATE)
        return pltpu.make_async_remote_copy(
            src_ref=mid_send.at[to], dst_ref=mid_recv.at[:, mid_at(origin), :],
            send_sem=mid_send_sem.at[k], recv_sem=mid_recv_sem.at[k],
            device_id={"seq": group * MID_RATE + to}, device_id_type=MESH,
        )

    def far_out_copy(k, origin):
        to = lax.rem(me + k, devices)
        return pltpu.make_async_remote_copy(
            src_ref=far_send.at[to], dst_ref=far_recv.at[origin],
            send_sem=far_send_sem.at[k], recv_sem=far_recv_sem.at[k],
            device_id={"seq": to}, device_id_type=MESH,
        )

    def mid_back_copy(k, origin):
        to = lax.rem(place + k, MID_RATE)
        return pltpu.make_async_remote_copy(
            src_ref=mid_res.at[mid_at(to), :], dst_ref=mid_back.at[origin],
            send_sem=mid_bs_sem.at[k], recv_sem=mid_br_sem.at[k],
            device_id={"seq": group * MID_RATE + to}, device_id_type=MESH,
        )

    def far_back_copy(k, origin):
        to = lax.rem(me + k, devices)
        return pltpu.make_async_remote_copy(
            src_ref=far_res.at[to], dst_ref=far_back.at[origin],
            send_sem=far_bs_sem.at[k], recv_sem=far_br_sem.at[k],
            device_id={"seq": to}, device_id_type=MESH,
        )

    def start_all(copy, mine, size):
        def one(k, carry):
            copy(k, mine).start()
            return carry

        lax.fori_loop(1, size, one, 0)

    def receive_all(copy, mine, size):
        def one(k, carry):
            copy(k, lax.rem(mine + size - k, size)).wait_recv()
            return carry

        lax.fori_loop(1, size, one, 0)

    def sent_all(copy, mine, size):
        def one(k, carry):
            copy(k, mine).wait_send()
            return carry

        lax.fori_loop(1, size, one, 0)

    start_all(far_out_copy, me, devices)
    start_all(mid_out_copy, place, MID_RATE)
    mid_recv[:, mid_at(place), :] = mid_send[place]
    far_recv[me] = far_send[me]

    def near_pair(g, carry):
        query, key, value = qkv[g], qkv[tiles_count + g], qkv[2 * tiles_count + g]
        one, one_top = head_attention(query, key, value, 0, bias[...], scale)
        two, two_top = head_attention(query, key, value, 1, bias[...], scale)
        near_r[g] = jnp.where(low, one, two)
        near_m[g] = jnp.where(low, one_top, two_top)
        return carry

    before = tiles_count - 3
    lax.fori_loop(0, before, near_pair, 0)

    inner = lane % SLOT
    piece = (SLOT - head_size) // 3
    places = (head_size, head_size + piece, head_size + 2 * piece)

    def packed(result, top, denom):
        total = top + jnp.log(denom) * LOG2E
        first = total.astype(jnp.bfloat16).astype(jnp.float32)
        second = (total - first).astype(jnp.bfloat16).astype(jnp.float32)
        third = total - first - second
        sums = jnp.where(inner < places[1], first, jnp.where(inner < places[2], second, third))
        return jnp.where(spare, sums, result / denom)

    def level_bias(offset, step, first):
        at = offset + step * (first + key_at)
        return jnp.where((at < count) | (query_at == key_at), 0.0, NEG)

    receive_all(far_out_copy, me, devices)
    both = far_recv[:, :far_rows, :].astype(jnp.float32).reshape(rows, LANES)
    folded = far_recv[:, far_rows:, :].astype(jnp.float32)
    far_value = jnp.concatenate([folded, swapped(folded)], axis=1).reshape(rows, LANES)
    result, top = head_attention(
        both.astype(jnp.bfloat16), swapped(both).astype(jnp.bfloat16),
        far_value.astype(jnp.bfloat16), 0, level_bias(me, devices, 0), scale,
    )
    result = packed(result, top, result[:, head_size : head_size + 1])
    result = result.reshape(devices, far_rows, LANES)
    far_res[...] = jnp.where(low[None], result[:, :fold], swapped(result[:, fold:])).astype(
        jnp.bfloat16
    )
    start_all(far_back_copy, me, devices)
    far_back[me] = far_res[me]

    receive_all(mid_out_copy, place, MID_RATE)
    halves = []
    for half in range(2):
        offset = lax.rem(2 * place + half, MID_RATE)
        result, top = head_attention(
            mid_recv[0], mid_recv[1], mid_recv[2], half,
            level_bias(offset, MID_RATE, group * rows), scale,
        )
        at = half * SLOT + head_size
        halves.append(packed(result, top, result[:, at : at + 1]))
    mid_res[...] = jnp.where(low, halves[0], halves[1]).astype(jnp.bfloat16)
    start_all(mid_back_copy, place, MID_RATE)
    mid_back[place] = mid_res[mid_at(place), :]

    lax.fori_loop(before, tiles_count, near_pair, 0)

    receive_all(mid_back_copy, place, MID_RATE)
    receive_all(far_back_copy, me, devices)

    def sum_of(tile):
        return jnp.where(
            low, tile[:, head_size : head_size + 1], tile[:, SLOT + head_size : SLOT + head_size + 1]
        )

    def log_of(tile):
        def at(half):
            return sum(tile[:, half * SLOT + i : half * SLOT + i + 1] for i in places)

        return jnp.where(low, at(0), at(1))

    def widen(tile, step):
        return jnp.broadcast_to(
            tile[:, None, :], (tile.shape[0], step, LANES)
        ).reshape(rows, LANES)

    def merge_pair(g, carry):
        head = 2 * g + jnp.where(low, 0, 1)
        one = far_back[2 * g].astype(jnp.float32)
        two = far_back[2 * g + 1].astype(jnp.float32)
        far = jnp.where(
            low,
            jnp.concatenate([one, swapped(one)], axis=0),
            jnp.concatenate([swapped(two), two], axis=0),
        )
        mid = mid_back[g].astype(jnp.float32)
        mid_on = row_id % MID_RATE == head % MID_RATE
        far_on = row_id % devices == head % devices
        near = near_r[g]
        tops = (
            near_m[g],
            jnp.where(mid_on, widen(log_of(mid), MID_RATE), NEG),
            jnp.where(far_on, widen(log_of(far), devices), NEG),
        )
        top = jnp.maximum(jnp.maximum(tops[0], tops[1]), tops[2])
        factors = [jnp.exp2(one - top) for one in tops]
        numer = (
            factors[0] * near
            + factors[1] * widen(mid, MID_RATE)
            + factors[2] * widen(far, devices)
        )
        denom = factors[0] * sum_of(near) + factors[1] + factors[2]
        att[g] = jnp.where(valid & jnp.logical_not(spare), numer / denom, 0.0).astype(jnp.bfloat16)
        return carry

    lax.fori_loop(0, tiles_count, merge_pair, 0)

    weight_copy(1).wait()
    for i in range(width // block):
        some = jnp.concatenate([att[i * per_block + j] for j in range(per_block)], axis=1)
        attended_ref[:, i * block : (i + 1) * block] = lax.dot_general(
            some, slots_ref[...], (((1,), (1,)), ((), ())), preferred_element_type=jnp.float32
        ).astype(jnp.bfloat16)
    for i in range(width // block):
        here = slice(i * block, (i + 1) * block)
        out = mixed[:, here] + jnp.dot(
            attended_ref[...], w_out_ref[:, here], preferred_element_type=jnp.float32
        )
        encoded_ref[:, here] = jnp.where(valid, out, 0.0).astype(jnp.bfloat16)

    @pl.when(me < devices - 1)
    def _():
        up_copy().wait_send()

    @pl.when(me > 0)
    def _():
        down_copy().wait_send()

    sent_all(mid_out_copy, place, MID_RATE)
    sent_all(far_out_copy, me, devices)
    sent_all(mid_back_copy, place, MID_RATE)
    sent_all(far_back_copy, me, devices)


def fused(tiles, tile_count, conv_weight, conv_bias, ln_gain, w_qkv, w_out):
    rows, width = tiles.shape
    devices = lax.axis_size("seq")
    head_size = width // ATTENTION_HEADS
    pairs = ATTENTION_HEADS // 2
    mid_rows, far_rows = rows // MID_RATE, rows // devices
    bf16, f32 = jnp.bfloat16, jnp.float32
    vmem = pl.BlockSpec(memory_space=pltpu.VMEM)
    anyspace = pl.BlockSpec(memory_space=pl.ANY)
    dma = pltpu.SemaphoreType.DMA
    return pl.pallas_call(
        functools.partial(layer_kernel, devices, head_size),
        out_shape=[jax.ShapeDtypeStruct((rows, width), bf16)] * 2,
        in_specs=[pl.BlockSpec(memory_space=pltpu.SMEM)] + [anyspace] * 6,
        out_specs=[vmem] * 2,
        scratch_shapes=[
            pltpu.VMEM((rows, width), bf16),
            pltpu.VMEM(conv_weight.shape, f32),
            pltpu.VMEM((width,), f32),
            pltpu.VMEM((width,), f32),
            pltpu.VMEM(w_qkv.shape, bf16),
            pltpu.VMEM(w_out.shape, bf16),
            pltpu.VMEM((HALO, width), bf16),
            pltpu.VMEM((HALO, width), bf16),
            pltpu.VMEM((rows + 2 * HALO + 2 * LEAD, width), f32),
            pltpu.VMEM((rows, width), f32),
            pltpu.VMEM((rows, width), bf16),
            pltpu.VMEM((3 * pairs, rows, LANES), f32),
            pltpu.VMEM((3 * pairs, rows, LANES), bf16),
            pltpu.VMEM((rows, rows), f32),
            pltpu.VMEM((pairs, rows, LANES), f32),
            pltpu.VMEM((pairs, rows, LANES), f32),
            pltpu.VMEM((pairs, 3, mid_rows, LANES), bf16),
            pltpu.VMEM((devices, 3 * far_rows // 2, LANES), bf16),
            pltpu.VMEM((3, rows, LANES), bf16),
            pltpu.VMEM((devices, 3 * far_rows // 2, LANES), bf16),
            pltpu.VMEM((rows, LANES), bf16),
            pltpu.VMEM((devices, far_rows // 2, LANES), bf16),
            pltpu.VMEM((pairs, mid_rows, LANES), bf16),
            pltpu.VMEM((devices, far_rows // 2, LANES), bf16),
            pltpu.VMEM((8 * head_size, 8 * SLOT), bf16),
            pltpu.VMEM((pairs, rows, LANES), bf16),
            dma((6,)), dma((2,)), dma((2,)),
            dma((MID_RATE,)), dma((MID_RATE,)), dma((devices,)), dma((devices,)),
            dma((MID_RATE,)), dma((MID_RATE,)), dma((devices,)), dma((devices,)),
        ],
        compiler_params=pltpu.CompilerParams(
            collective_id=0, has_side_effects=True, vmem_limit_bytes=50 * 1024 * 1024
        ),
    )(tile_count, tiles, conv_weight, conv_bias, ln_gain, w_qkv, w_out)


def solution(mesh):
    placed = (P(("slides", "seq"), None), P("slides"), P(), P(), P(), P(), P())
    body = fused if mesh.shape["seq"] == ATTENTION_HEADS else shards
    return jax.shard_map(
        body,
        mesh=mesh,
        in_specs=placed,
        out_specs=(P(("slides", "seq"), None), P(("slides", "seq"), None)),
        check_vma=False,
    )
```

```python
import functools

import jax
import jax.numpy as jnp
from jax import lax
from jax.experimental import pallas as pl
from jax.experimental.pallas import tpu as pltpu
from jax.sharding import PartitionSpec as P

ATTENTION_HEADS = 16
GW = 128
MID_RATE = 8


EPS = 1e-05
NEG = -1e30


def extended(block, sides, width):
    for axis, dim in sides:
        count = lax.axis_size(axis)
        forward = [(i, i + 1) for i in range(count - 1)]
        backward = [(target, source) for source, target in forward]
        low = lax.ppermute(
            lax.slice_in_dim(block, block.shape[dim] - width, None, axis=dim), axis, forward
        )
        high = lax.ppermute(lax.slice_in_dim(block, 0, width, axis=dim), axis, backward)
        block = jnp.concatenate([low, block, high], axis=dim)
    return block


def permitted_mask(query_index, key_index, dilation_step, active_count, head_total):
    shift_amounts = jnp.arange(head_total, dtype=jnp.int32) % dilation_step
    key_position = shift_amounts[:, None] + dilation_step * key_index[None, :]
    key_live = key_position < active_count
    return key_live[:, None, :] | (query_index[None, :, None] == key_index[None, None, :])


def attend_single_block(query_portion, key_portion, value_portion, allowed):
    score_scale = query_portion.shape[2] ** (-0.5)
    scores = (
        jnp.einsum("qhd,khd->hqk", query_portion, key_portion, preferred_element_type=jnp.float32)
        * score_scale
    )
    scores = jnp.where(allowed, scores, NEG)
    row_top = jnp.max(scores, axis=2, keepdims=True)
    exp_terms = jnp.where(allowed, jnp.exp(scores - row_top), 0.0)
    denom_sum = jnp.sum(exp_terms, axis=2)
    weights = exp_terms.astype(jnp.bfloat16)
    summed = jnp.einsum("hqk,khd->qhd", weights, value_portion, preferred_element_type=jnp.float32)
    level_lse = jnp.transpose(row_top[:, :, 0] + jnp.log(denom_sum))
    return (summed / jnp.transpose(denom_sum)[:, :, None], level_lse)


def offset_keep(dilation_step, model_width, head_size):
    step_index = jnp.arange(dilation_step, dtype=jnp.int32)[:, None]
    column_head = jnp.arange(model_width, dtype=jnp.int32)[None, :] // head_size
    return step_index == column_head % dilation_step


def dilated_rows(source_rows, dilation_step, head_size):
    model_width = source_rows.shape[1]
    grouped_rows = source_rows.reshape(
        source_rows.shape[0] // dilation_step, dilation_step, model_width
    )
    keep = offset_keep(dilation_step, model_width, head_size)
    return jnp.sum(jnp.where(keep[None], grouped_rows, jnp.zeros((), source_rows.dtype)), axis=1)


def scatter_back(sparse_output, sparse_logsumexp, dilation_step, head_size):
    sparse_rows, heads_total = sparse_logsumexp.shape
    model_width = heads_total * head_size
    flat_out = sparse_output.reshape(sparse_rows, model_width)
    keep = offset_keep(dilation_step, model_width, head_size)
    widened = jnp.where(keep[None], flat_out[:, None, :], 0.0)
    match_flag = (
        jnp.arange(dilation_step)[:, None] == (jnp.arange(heads_total) % dilation_step)[None, :]
    )
    lse_wide = jnp.where(match_flag[None], sparse_logsumexp[:, None, :], NEG)
    output_rows = sparse_rows * dilation_step
    return (
        widened.reshape(output_rows, heads_total, head_size),
        lse_wide.reshape(output_rows, heads_total),
    )


def merge_levels(level_outs, level_lses):
    top_all = jnp.maximum(jnp.maximum(level_lses[0], level_lses[1]), level_lses[2])
    factors = [jnp.exp(one_lse - top_all) for one_lse in level_lses]
    numer = (
        factors[0][:, :, None] * level_outs[0]
        + factors[1][:, :, None] * level_outs[1]
        + factors[2][:, :, None] * level_outs[2]
    )
    return numer / (factors[0] + factors[1] + factors[2])[:, :, None]


def positional_sum(padded, column, conv_weight, halo_width, out_rows):
    summed = jnp.zeros((out_rows, padded.shape[1]), jnp.float32)
    for row_step in range(-2, 3):
        for col_step in range(-2, 3):
            start_row = halo_width + row_step * GW + col_step
            window = padded[start_row : start_row + out_rows].astype(jnp.float32)
            inside = ((column + col_step >= 0) & (column + col_step < GW)).astype(jnp.float32)
            summed = summed + window * (
                conv_weight[(row_step + 2) * 5 + col_step + 2][None, :] * inside[:, None]
            )
    return summed


def normalize(mixed_in, ln_gain):
    row_mean = jnp.mean(mixed_in, axis=1, keepdims=True)
    centred = mixed_in - row_mean
    row_var = jnp.mean(centred * centred, axis=1, keepdims=True)
    return (centred * lax.rsqrt(row_var + EPS) * ln_gain).astype(jnp.bfloat16)


def shards(tiles, tile_count, conv_weight, conv_bias, ln_gain, w_qkv, w_out):
    local_rows = tiles.shape[0]
    model_width = tiles.shape[1]
    head_size = model_width // ATTENTION_HEADS
    devices = lax.axis_size("seq")
    dev_index = lax.axis_index("seq")
    active_count = tile_count[0]
    position = dev_index * local_rows + jnp.arange(local_rows, dtype=jnp.int32)
    valid_row = (position < active_count).astype(jnp.float32)[:, None]
    masked = tiles * valid_row.astype(jnp.bfloat16)
    halo_width = 2 * GW + 2
    padded = extended(masked, (("seq", 0),), halo_width)
    column = jnp.arange(local_rows, dtype=jnp.int32) % GW
    summed = positional_sum(padded, column, conv_weight, halo_width, local_rows)
    mixed_in = (masked.astype(jnp.float32) + summed + conv_bias) * valid_row
    normed = normalize(mixed_in, ln_gain)
    projected = jnp.dot(normed, w_qkv, preferred_element_type=jnp.float32).astype(jnp.bfloat16)
    query_flat = projected[:, :model_width]
    key_flat = projected[:, model_width : 2 * model_width]
    value_flat = projected[:, 2 * model_width :]

    def heads_of(flat_rows):
        return flat_rows.reshape(flat_rows.shape[0], ATTENTION_HEADS, head_size)

    near_out, near_lse = attend_single_block(
        heads_of(query_flat),
        heads_of(key_flat),
        heads_of(value_flat),
        permitted_mask(position, position, 1, active_count, ATTENTION_HEADS),
    )
    mid_rows = local_rows // MID_RATE
    mid_query = heads_of(dilated_rows(query_flat, MID_RATE, head_size))
    mid_kv = jnp.stack(
        [dilated_rows(key_flat, MID_RATE, head_size), dilated_rows(value_flat, MID_RATE, head_size)]
    )
    mid_query_idx = dev_index * mid_rows + jnp.arange(mid_rows, dtype=jnp.int32)
    group_base = dev_index // MID_RATE * local_rows
    far_rows = local_rows // devices
    far_query = heads_of(dilated_rows(query_flat, devices, head_size))
    far_kv = jnp.stack(
        [dilated_rows(key_flat, devices, head_size), dilated_rows(value_flat, devices, head_size)]
    )
    far_query_idx = dev_index * far_rows + jnp.arange(far_rows, dtype=jnp.int32)
    mid_all, far_all = (
        lax.all_gather(mid_kv, "seq", axis=1, tiled=True),
        lax.all_gather(far_kv, "seq", axis=1, tiled=True),
    )
    group_kv = lax.dynamic_slice_in_dim(mid_all, group_base, local_rows, 1)
    far_keys_idx = jnp.arange(local_rows, dtype=jnp.int32)
    far_sparse, far_sparse_lse = attend_single_block(
        far_query,
        heads_of(far_all[0]),
        heads_of(far_all[1]),
        permitted_mask(far_query_idx, far_keys_idx, devices, active_count, ATTENTION_HEADS),
    )
    group_idx = group_base + jnp.arange(local_rows, dtype=jnp.int32)
    mid_sparse, mid_sparse_lse = attend_single_block(
        mid_query,
        heads_of(group_kv[0]),
        heads_of(group_kv[1]),
        permitted_mask(mid_query_idx, group_idx, MID_RATE, active_count, ATTENTION_HEADS),
    )
    mid_out, mid_lse = scatter_back(mid_sparse, mid_sparse_lse, MID_RATE, head_size)
    far_out, far_lse = scatter_back(far_sparse, far_sparse_lse, devices, head_size)
    heads_all = merge_levels((near_out, mid_out, far_out), (near_lse, mid_lse, far_lse))
    attended = (heads_all.reshape(local_rows, model_width) * valid_row).astype(jnp.bfloat16)
    encoded = (
        (mixed_in + jnp.dot(attended, w_out, preferred_element_type=jnp.float32)) * valid_row
    ).astype(jnp.bfloat16)
    return (attended, encoded)


MESH = pl.DeviceIdType.MESH
LOG2E = 1.4426950408889634
LANES = 128
SLOT = 64
HALO = 2 * GW
LEAD = 8


def head_slots(model_width, head_size):
    packed = 8 * head_size
    slotted = 8 * SLOT
    source = lax.broadcasted_iota(jnp.int32, (packed, slotted), 0)
    target = lax.broadcasted_iota(jnp.int32, (packed, slotted), 1)
    inner = target % SLOT
    match = (inner < head_size) & (source == (target // SLOT) * head_size + inner)
    return jnp.where(match, 1.0, 0.0).astype(jnp.bfloat16)


def head_attention(query, key, value, half, bias, scale):
    lane = lax.broadcasted_iota(jnp.int32, query.shape, 1)
    own = jnp.where(lane // SLOT == half, query, jnp.zeros((), query.dtype))
    scores = lax.dot_general(
        own, key, (((1,), (1,)), ((), ())), preferred_element_type=jnp.float32
    )
    scores = scores * scale + bias
    top = jnp.max(scores, axis=1, keepdims=True)
    weights = jnp.exp2(scores - top).astype(jnp.bfloat16)
    return jnp.dot(weights, value, preferred_element_type=jnp.float32), top


def layer_kernel(
    devices, head_size,
    count_ref, tiles_hbm, conv_w_hbm, conv_b_hbm, gain_hbm, w_qkv_hbm, w_out_hbm,
    attended_ref, encoded_ref,
    tiles_ref, conv_w_ref, conv_b_ref, gain_ref, w_qkv_ref, w_out_ref, halo_lo, halo_hi, ext, mixed, normed, qkv_wide, qkv, bias,
    near_r, near_m, mid_send, far_send, mid_recv, far_recv, mid_res, far_res,
    mid_back, far_back, slots_ref, att,
    w_sem, halo_send_sem, halo_recv_sem, mid_send_sem, mid_recv_sem, far_send_sem, far_recv_sem,
    mid_bs_sem, mid_br_sem, far_bs_sem, far_br_sem,
):
    rows, width = tiles_ref.shape
    me = lax.axis_index("seq")
    group = me // MID_RATE
    place = lax.rem(me, MID_RATE)
    mid_rows = rows // MID_RATE
    far_rows = rows // devices
    tiles_count = ATTENTION_HEADS // 2
    grid_rows = rows // GW
    scale = head_size ** (-0.5) * LOG2E
    count = count_ref[0]

    def weight_copy(i):
        source, target = (
            (w_qkv_hbm, w_qkv_ref), (w_out_hbm, w_out_ref), (tiles_hbm, tiles_ref),
            (conv_w_hbm, conv_w_ref), (conv_b_hbm, conv_b_ref), (gain_hbm, gain_ref),
        )[i]
        return pltpu.make_async_copy(source, target, w_sem.at[i])

    for i in (2, 3, 4, 5, 0, 1):
        weight_copy(i).start()

    barrier = pltpu.get_barrier_semaphore()

    def greet(k, carry):
        pl.semaphore_signal(
            barrier, inc=1, device_id={"seq": lax.rem(me + k, devices)}, device_id_type=MESH
        )
        return carry

    lax.fori_loop(1, devices, greet, 0)

    base = me * rows
    row_id = lax.broadcasted_iota(jnp.int32, (rows, 1), 0)
    valid = base + row_id < count

    def masked_of(block, first):
        at = first + lax.broadcasted_iota(jnp.int32, (block.shape[0], 1), 0)
        return jnp.where((at >= 0) & (at < count), block.astype(jnp.float32), 0.0)

    ext[0:LEAD, :] = jnp.zeros((LEAD, width), jnp.float32)
    ext[LEAD + 2 * HALO + rows :, :] = jnp.zeros((LEAD, width), jnp.float32)
    ext[LEAD : LEAD + HALO, :] = jnp.zeros((HALO, width), jnp.float32)
    ext[LEAD + HALO + rows : LEAD + 2 * HALO + rows, :] = jnp.zeros((HALO, width), jnp.float32)
    pl.semaphore_wait(barrier, devices - 1)

    def up_copy():
        return pltpu.make_async_remote_copy(
            src_ref=tiles_hbm.at[pl.ds(rows - HALO, HALO), :], dst_ref=halo_lo,
            send_sem=halo_send_sem.at[0], recv_sem=halo_recv_sem.at[0],
            device_id={"seq": me + 1}, device_id_type=MESH,
        )

    def down_copy():
        return pltpu.make_async_remote_copy(
            src_ref=tiles_hbm.at[pl.ds(0, HALO), :], dst_ref=halo_hi,
            send_sem=halo_send_sem.at[1], recv_sem=halo_recv_sem.at[1],
            device_id={"seq": me - 1}, device_id_type=MESH,
        )

    @pl.when(me < devices - 1)
    def _():
        up_copy().start()

    @pl.when(me > 0)
    def _():
        down_copy().start()

    for i in (2, 3, 4, 5):
        weight_copy(i).wait()
    ext[LEAD + HALO : LEAD + HALO + rows, :] = masked_of(tiles_ref[...], base)
    slots_ref[...] = head_slots(width, head_size)
    key_at = lax.broadcasted_iota(jnp.int32, (rows, rows), 1)
    query_at = lax.broadcasted_iota(jnp.int32, (rows, rows), 0)
    bias[...] = jnp.where((base + key_at < count) | (query_at == key_at), 0.0, NEG)

    column = lax.broadcasted_iota(jnp.int32, (GW, LANES), 0)

    def conv_rows(r, row_steps, lanes, total):
        for b in range(-2, 3):
            part = None
            for a in row_steps:
                start = LEAD + HALO + (r + a) * GW + b
                term = ext[start : start + GW, lanes] * conv_w_ref[
                    (a + 2) * 5 + b + 2 : (a + 2) * 5 + b + 3, lanes
                ]
                part = term if part is None else part + term
            if b != 0:
                part = jnp.where((column + b >= 0) & (column + b < GW), part, 0.0)
            total = total + part
        return total

    def inner_conv(t, carry):
        lanes = pl.ds(pl.multiple_of(t * LANES, LANES), LANES)
        for r in range(grid_rows):
            here = slice(r * GW, (r + 1) * GW)
            start = LEAD + HALO + r * GW
            total = ext[start : start + GW, lanes] + conv_b_ref[lanes][None]
            steps = [a for a in range(-2, 3) if 0 <= r + a < grid_rows]
            mixed[here, lanes] = conv_rows(r, steps, lanes, total)
        return carry

    lax.fori_loop(0, width // LANES, inner_conv, 0)

    @pl.when(me > 0)
    def _():
        up_copy().wait_recv()
        ext[LEAD : LEAD + HALO, :] = masked_of(halo_lo[...], base - HALO)

    @pl.when(me < devices - 1)
    def _():
        down_copy().wait_recv()
        ext[LEAD + HALO + rows : LEAD + 2 * HALO + rows, :] = masked_of(halo_hi[...], base + rows)

    def outer_conv(t, carry):
        lanes = pl.ds(pl.multiple_of(t * LANES, LANES), LANES)
        for r in range(grid_rows):
            here = slice(r * GW, (r + 1) * GW)
            steps = [a for a in range(-2, 3) if not 0 <= r + a < grid_rows]
            mixed[here, lanes] = jnp.where(
                base + r * GW + column < count,
                conv_rows(r, steps, lanes, mixed[here, lanes]) if steps else mixed[here, lanes],
                0.0,
            )
        return carry

    lax.fori_loop(0, width // LANES, outer_conv, 0)

    def norm_rows(i, carry):
        here = pl.ds(pl.multiple_of(i * GW, GW), GW)
        x = mixed[here, :]
        centred = x - jnp.mean(x, axis=1, keepdims=True)
        var = jnp.mean(centred * centred, axis=1, keepdims=True)
        normed[here, :] = (centred * lax.rsqrt(var + EPS) * gain_ref[...][None]).astype(jnp.bfloat16)
        return carry

    lax.fori_loop(0, grid_rows, norm_rows, 0)

    lane = lax.broadcasted_iota(jnp.int32, (1, LANES), 1)
    spare = lane % SLOT >= head_size
    low = lane < SLOT
    weight_copy(0).wait()
    block = 8 * head_size
    per_block = 8 * SLOT // LANES

    for b in range(3 * width // block):
        some = jnp.dot(
            normed[...], w_qkv_ref[:, b * block : (b + 1) * block],
            preferred_element_type=jnp.float32,
        ).astype(jnp.bfloat16)
        spread = jnp.dot(some, slots_ref[...], preferred_element_type=jnp.float32)
        for i in range(per_block):
            tile = spread[:, i * LANES : (i + 1) * LANES]
            if b * block >= 2 * width:
                tile = jnp.where(spare, 1.0, tile)
            qkv_wide[b * per_block + i] = tile
            qkv[b * per_block + i] = tile.astype(jnp.bfloat16)

    fold = far_rows // 2

    def swapped(x):
        return pltpu.roll(x, SLOT, x.ndim - 1)

    for g in range(tiles_count):
        for c in range(3):
            from_tile = c * tiles_count + g

            one = qkv_wide[from_tile, pl.ds((2 * g) % MID_RATE, mid_rows, stride=MID_RATE), :]
            two = qkv_wide[from_tile, pl.ds((2 * g + 1) % MID_RATE, mid_rows, stride=MID_RATE), :]
            mid_send[g, c] = jnp.where(low, one, two).astype(jnp.bfloat16)
        for half in range(2):
            query, key, value = (
                qkv_wide[c * tiles_count + g, pl.ds(2 * g + half, far_rows, stride=devices), :]
                for c in range(3)
            )
            if half == 0:
                key, last = swapped(key), swapped(value[fold:])
                first = value[:fold]
            else:
                query, first = swapped(query), swapped(value[:fold])
                last = value[fold:]
            far_send[2 * g + half, :far_rows] = jnp.where(low, query, key).astype(jnp.bfloat16)
            far_send[2 * g + half, far_rows:] = jnp.where(low, first, last).astype(jnp.bfloat16)

    def mid_at(index):
        return pl.ds(pl.multiple_of(index * mid_rows, mid_rows), mid_rows)

    def mid_out_copy(k, origin):
        to = lax.rem(place + k, MID_RATE)
        return pltpu.make_async_remote_copy(
            src_ref=mid_send.at[to], dst_ref=mid_recv.at[:, mid_at(origin), :],
            send_sem=mid_send_sem.at[k], recv_sem=mid_recv_sem.at[k],
            device_id={"seq": group * MID_RATE + to}, device_id_type=MESH,
        )

    def far_out_copy(k, origin):
        to = lax.rem(me + k, devices)
        return pltpu.make_async_remote_copy(
            src_ref=far_send.at[to], dst_ref=far_recv.at[origin],
            send_sem=far_send_sem.at[k], recv_sem=far_recv_sem.at[k],
            device_id={"seq": to}, device_id_type=MESH,
        )

    def mid_back_copy(k, origin):
        to = lax.rem(place + k, MID_RATE)
        return pltpu.make_async_remote_copy(
            src_ref=mid_res.at[mid_at(to), :], dst_ref=mid_back.at[origin],
            send_sem=mid_bs_sem.at[k], recv_sem=mid_br_sem.at[k],
            device_id={"seq": group * MID_RATE + to}, device_id_type=MESH,
        )

    def far_back_copy(k, origin):
        to = lax.rem(me + k, devices)
        return pltpu.make_async_remote_copy(
            src_ref=far_res.at[to], dst_ref=far_back.at[origin],
            send_sem=far_bs_sem.at[k], recv_sem=far_br_sem.at[k],
            device_id={"seq": to}, device_id_type=MESH,
        )

    def start_all(copy, mine, size):
        def one(k, carry):
            copy(k, mine).start()
            return carry

        lax.fori_loop(1, size, one, 0)

    def receive_all(copy, mine, size):
        def one(k, carry):
            copy(k, lax.rem(mine + size - k, size)).wait_recv()
            return carry

        lax.fori_loop(1, size, one, 0)

    def sent_all(copy, mine, size):
        def one(k, carry):
            copy(k, mine).wait_send()
            return carry

        lax.fori_loop(1, size, one, 0)

    start_all(far_out_copy, me, devices)
    start_all(mid_out_copy, place, MID_RATE)
    mid_recv[:, mid_at(place), :] = mid_send[place]
    far_recv[me] = far_send[me]

    def near_pair(g, carry):
        query, key, value = qkv[g], qkv[tiles_count + g], qkv[2 * tiles_count + g]
        one, one_top = head_attention(query, key, value, 0, bias[...], scale)
        two, two_top = head_attention(query, key, value, 1, bias[...], scale)
        near_r[g] = jnp.where(low, one, two)
        near_m[g] = jnp.where(low, one_top, two_top)
        return carry

    before = tiles_count - 3
    lax.fori_loop(0, before, near_pair, 0)

    inner = lane % SLOT
    piece = (SLOT - head_size) // 3
    places = (head_size, head_size + piece, head_size + 2 * piece)

    def packed(result, top, denom):
        total = top + jnp.log(denom) * LOG2E
        first = total.astype(jnp.bfloat16).astype(jnp.float32)
        second = (total - first).astype(jnp.bfloat16).astype(jnp.float32)
        third = total - first - second
        sums = jnp.where(inner < places[1], first, jnp.where(inner < places[2], second, third))
        return jnp.where(spare, sums, result / denom)

    def level_bias(offset, step, first):
        at = offset + step * (first + key_at)
        return jnp.where((at < count) | (query_at == key_at), 0.0, NEG)

    receive_all(far_out_copy, me, devices)
    both = far_recv[:, :far_rows, :].astype(jnp.float32).reshape(rows, LANES)
    folded = far_recv[:, far_rows:, :].astype(jnp.float32)
    far_value = jnp.concatenate([folded, swapped(folded)], axis=1).reshape(rows, LANES)
    result, top = head_attention(
        both.astype(jnp.bfloat16), swapped(both).astype(jnp.bfloat16),
        far_value.astype(jnp.bfloat16), 0, level_bias(me, devices, 0), scale,
    )
    result = packed(result, top, result[:, head_size : head_size + 1])
    result = result.reshape(devices, far_rows, LANES)
    far_res[...] = jnp.where(low[None], result[:, :fold], swapped(result[:, fold:])).astype(
        jnp.bfloat16
    )
    start_all(far_back_copy, me, devices)
    far_back[me] = far_res[me]

    receive_all(mid_out_copy, place, MID_RATE)
    halves = []
    for half in range(2):
        offset = lax.rem(2 * place + half, MID_RATE)
        result, top = head_attention(
            mid_recv[0], mid_recv[1], mid_recv[2], half,
            level_bias(offset, MID_RATE, group * rows), scale,
        )
        at = half * SLOT + head_size
        halves.append(packed(result, top, result[:, at : at + 1]))
    mid_res[...] = jnp.where(low, halves[0], halves[1]).astype(jnp.bfloat16)
    start_all(mid_back_copy, place, MID_RATE)
    mid_back[place] = mid_res[mid_at(place), :]

    lax.fori_loop(before, tiles_count, near_pair, 0)

    receive_all(mid_back_copy, place, MID_RATE)
    receive_all(far_back_copy, me, devices)

    def sum_of(tile):
        return jnp.where(
            low, tile[:, head_size : head_size + 1], tile[:, SLOT + head_size : SLOT + head_size + 1]
        )

    def log_of(tile):
        def at(half):
            return sum(tile[:, half * SLOT + i : half * SLOT + i + 1] for i in places)

        return jnp.where(low, at(0), at(1))

    def widen(tile, step):
        return jnp.broadcast_to(
            tile[:, None, :], (tile.shape[0], step, LANES)
        ).reshape(rows, LANES)

    def merge_pair(g, carry):
        head = 2 * g + jnp.where(low, 0, 1)
        one = far_back[2 * g].astype(jnp.float32)
        two = far_back[2 * g + 1].astype(jnp.float32)
        far = jnp.where(
            low,
            jnp.concatenate([one, swapped(one)], axis=0),
            jnp.concatenate([swapped(two), two], axis=0),
        )
        mid = mid_back[g].astype(jnp.float32)
        mid_on = row_id % MID_RATE == head % MID_RATE
        far_on = row_id % devices == head % devices
        near = near_r[g]
        tops = (
            near_m[g],
            jnp.where(mid_on, widen(log_of(mid), MID_RATE), NEG),
            jnp.where(far_on, widen(log_of(far), devices), NEG),
        )
        top = jnp.maximum(jnp.maximum(tops[0], tops[1]), tops[2])
        factors = [jnp.exp2(one - top) for one in tops]
        numer = (
            factors[0] * near
            + factors[1] * widen(mid, MID_RATE)
            + factors[2] * widen(far, devices)
        )
        denom = factors[0] * sum_of(near) + factors[1] + factors[2]
        att[g] = jnp.where(valid & jnp.logical_not(spare), numer / denom, 0.0).astype(jnp.bfloat16)
        return carry

    lax.fori_loop(0, tiles_count, merge_pair, 0)

    weight_copy(1).wait()
    for i in range(width // block):
        some = jnp.concatenate([att[i * per_block + j] for j in range(per_block)], axis=1)
        attended_ref[:, i * block : (i + 1) * block] = lax.dot_general(
            some, slots_ref[...], (((1,), (1,)), ((), ())), preferred_element_type=jnp.float32
        ).astype(jnp.bfloat16)
    for i in range(width // block):
        here = slice(i * block, (i + 1) * block)
        out = mixed[:, here] + jnp.dot(
            attended_ref[...], w_out_ref[:, here], preferred_element_type=jnp.float32
        )
        encoded_ref[:, here] = jnp.where(valid, out, 0.0).astype(jnp.bfloat16)

    @pl.when(me < devices - 1)
    def _():
        up_copy().wait_send()

    @pl.when(me > 0)
    def _():
        down_copy().wait_send()

    sent_all(mid_out_copy, place, MID_RATE)
    sent_all(far_out_copy, me, devices)
    sent_all(mid_back_copy, place, MID_RATE)
    sent_all(far_back_copy, me, devices)


def fused(tiles, tile_count, conv_weight, conv_bias, ln_gain, w_qkv, w_out):
    rows, width = tiles.shape
    devices = lax.axis_size("seq")
    head_size = width // ATTENTION_HEADS
    pairs = ATTENTION_HEADS // 2
    mid_rows, far_rows = rows // MID_RATE, rows // devices
    bf16, f32 = jnp.bfloat16, jnp.float32
    vmem = pl.BlockSpec(memory_space=pltpu.VMEM)
    hbm = pl.BlockSpec(memory_space=pltpu.HBM)
    dma = pltpu.SemaphoreType.DMA
    return pl.pallas_call(
        functools.partial(layer_kernel, devices, head_size),
        out_shape=[jax.ShapeDtypeStruct((rows, width), bf16)] * 2,
        in_specs=[pl.BlockSpec(memory_space=pltpu.SMEM)] + [hbm] * 6,
        out_specs=[vmem] * 2,
        scratch_shapes=[
            pltpu.VMEM((rows, width), bf16),
            pltpu.VMEM(conv_weight.shape, f32),
            pltpu.VMEM((width,), f32),
            pltpu.VMEM((width,), f32),
            pltpu.VMEM(w_qkv.shape, bf16),
            pltpu.VMEM(w_out.shape, bf16),
            pltpu.VMEM((HALO, width), bf16),
            pltpu.VMEM((HALO, width), bf16),
            pltpu.VMEM((rows + 2 * HALO + 2 * LEAD, width), f32),
            pltpu.VMEM((rows, width), f32),
            pltpu.VMEM((rows, width), bf16),
            pltpu.VMEM((3 * pairs, rows, LANES), f32),
            pltpu.VMEM((3 * pairs, rows, LANES), bf16),
            pltpu.VMEM((rows, rows), f32),
            pltpu.VMEM((pairs, rows, LANES), f32),
            pltpu.VMEM((pairs, rows, LANES), f32),
            pltpu.VMEM((pairs, 3, mid_rows, LANES), bf16),
            pltpu.VMEM((devices, 3 * far_rows // 2, LANES), bf16),
            pltpu.VMEM((3, rows, LANES), bf16),
            pltpu.VMEM((devices, 3 * far_rows // 2, LANES), bf16),
            pltpu.VMEM((rows, LANES), bf16),
            pltpu.VMEM((devices, far_rows // 2, LANES), bf16),
            pltpu.VMEM((pairs, mid_rows, LANES), bf16),
            pltpu.VMEM((devices, far_rows // 2, LANES), bf16),
            pltpu.VMEM((8 * head_size, 8 * SLOT), bf16),
            pltpu.VMEM((pairs, rows, LANES), bf16),
            dma((6,)), dma((2,)), dma((2,)),
            dma((MID_RATE,)), dma((MID_RATE,)), dma((devices,)), dma((devices,)),
            dma((MID_RATE,)), dma((MID_RATE,)), dma((devices,)), dma((devices,)),
        ],
        compiler_params=pltpu.CompilerParams(
            collective_id=0, has_side_effects=True, vmem_limit_bytes=60 * 1024 * 1024
        ),
    )(tile_count, tiles, conv_weight, conv_bias, ln_gain, w_qkv, w_out)


def solution(mesh):
    placed = (P(("slides", "seq"), None), P("slides"), P(), P(), P(), P(), P())
    body = fused if mesh.shape["seq"] == ATTENTION_HEADS else shards
    return jax.shard_map(
        body,
        mesh=mesh,
        in_specs=placed,
        out_specs=(P(("slides", "seq"), None), P(("slides", "seq"), None)),
        check_vma=False,
    )
```
